512 devices in a mesh: seq: 32 (over z, core), mp: 16 (over x, y).
Axes of the slice: x: 4, y: 4, z: 16, core: 2. Of those that a mesh axis runs over, the one named last changes fastest.
Arguments:
- qkv: bfloat16 [3, 65536, 4096], P(None, ('seq', 'mp')), may hold values from -6 to 6
- pack_segments: int32 [32, 64], replicated, may hold values from 0 to 63, as said below
- slot_offset: int32 [32], replicated, may hold values from 0 to 31, as said below
Outputs:
- attended: bfloat16 [65536, 4096], P('seq', 'mp')
The draws below stay inside these ranges and needn't reach their ends.
Inputs may be any that keep to these rules, and one draw needn't show every extreme that they name: `pack_segments`: row p lists, for the 64 blocks of 32 tokens of pack p, the number of the image that each block belongs to: 0 for the first block, rising by one at each new image. An image has 1 or 2 blocks, and one of 2 blocks starts at an even block. `slot_offset`: each value once.
All inputs are finite; a program needn't handle non-finite values.
Results may differ from the reference program's by a relative error of at most 0.0047.
Values may be sent and summed in bfloat16 or wider, within the bound.
A program may use at most 64 MiB of HBM per device.

```python
import math
import jax
import jax.numpy as jnp
from jax import lax

HEAD = 128
HEADS = 32
TOK_DEV = 2048
BLOCK = 32
PAIR = 64
SLOTS = 32
PACK_BLOCKS = 64
PACKS = 32
TOKENS = 65536


def draw_qkv(key, part):
    key = jax.random.fold_in(key, 11)
    base_key, scale_key = jax.random.split(key, 2)
    feature_width = HEADS * HEAD
    shape = (3, TOKENS, feature_width)
    row_scale = jnp.exp(jax.random.uniform(scale_key, (3, TOKENS, 1), minval=math.log(0.4), maxval=math.log(2.4)))
    values = jnp.clip(jax.random.normal(base_key, shape), -2.4, 2.4) * row_scale
    return values.astype(jnp.bfloat16)


def draw_pack_segments(key, part):
    key = jax.random.fold_in(key, 12)
    level_key, split_key, full_key = jax.random.split(key, 3)
    level = jax.random.randint(level_key, (PACKS, 1), 0, 5)
    split_draw = jax.random.randint(split_key, (PACKS, SLOTS), 0, 4)
    splits = (split_draw < level).astype(jnp.int32)
    full_pack = jax.random.randint(full_key, (), 0, PACKS)
    splits = jnp.where(jnp.arange(PACKS)[:, None] == full_pack, 1, splits).astype(jnp.int32)
    firsts = jnp.cumsum(1 + splits, axis=1) - (1 + splits)
    seconds = firsts + splits
    return jnp.stack([firsts, seconds], axis=2).reshape(PACKS, PACK_BLOCKS).astype(jnp.int32)


def draw_slot_offset(key, part):
    key = jax.random.fold_in(key, 13)
    return jax.random.permutation(key, PACKS)[:SLOTS].astype(jnp.int32)


def setup_inputs(seed: int = 0) -> dict:
    streams_of = jax.random.split(jax.random.key(seed), 4)
    qkv = draw_qkv(jax.random.fold_in(streams_of[3], 71), 0)
    pack_segments = draw_pack_segments(jax.random.fold_in(streams_of[3], 71), 0)
    slot_offset = draw_slot_offset(jax.random.fold_in(streams_of[3], 71), 0)
    return dict(qkv=qkv, pack_segments=pack_segments, slot_offset=slot_offset)


def reference(qkv, pack_segments, slot_offset):
    feature_width = HEADS * HEAD
    slot_ids = jnp.arange(SLOTS, dtype=jnp.int32)
    pair_ids = jnp.arange(PAIR, dtype=jnp.int32)

    def one_pack(pack_index):
        loaders = ((pack_index + slot_offset) % PACKS).astype(jnp.int32)
        first_rows = loaders * TOK_DEV + slot_ids * PAIR
        row_ids = (first_rows[:, None] + pair_ids[None, :]).reshape(-1).astype(jnp.int32)
        gathered = jnp.take(qkv, row_ids, axis=1)
        gathered = gathered.astype(jnp.float32).reshape(3, SLOTS, PAIR, HEADS, HEAD)
        segment = jnp.repeat(pack_segments[pack_index], BLOCK).reshape(SLOTS, PAIR)
        same_image = segment[:, :, None] == segment[:, None, :]
        scores = jnp.einsum("sqhd,skhd->shqk", gathered[0], gathered[1]) * (HEAD ** -0.5)
        scores = jnp.where(same_image[:, None], scores, -jnp.inf)
        weights = jax.nn.softmax(scores, axis=-1).astype(jnp.bfloat16)
        weights = lax.optimization_barrier(weights).astype(jnp.float32)
        result = jnp.einsum("shqk,skhd->sqhd", weights, gathered[2])
        return result.reshape(TOK_DEV, feature_width).astype(jnp.bfloat16)

    packs_out = lax.map(one_pack, jnp.arange(PACKS, dtype=jnp.int32))
    return packs_out.reshape(TOKENS, feature_width)
```

```python
import functools
import math

import jax
import jax.numpy as jnp
from jax import lax
from jax.experimental import pallas as pl
from jax.experimental.pallas import tpu as pltpu
from jax.sharding import PartitionSpec as P

HEAD = 128
LOG2E = 1.4426950408889634
MESH = pl.DeviceIdType.MESH
SPLIT = 2
UNROLL = 4


def ring_peer(own, step, count):
    chips = count // 2
    k = step // 2
    away = chips // 2 - (k + 1) // 2
    turn = jnp.where(k % 2 == 1, away, chips - away)
    chip = (own // 2 + turn) % chips
    return 2 * chip + (own + step + 1) % 2


def kernel(
    seqs, mps, offset_ref, segment_ref, qkv_ref, out_ref,
    qkv_v, first_out, second_out, result, slot_v, slot_s,
    load_sem, slot_sem, first_send, first_recv, second_send, second_recv, out_sem, *landing,
):
    first_in, second_in = landing[:len(landing) // 2], landing[len(landing) // 2:]
    me = lax.axis_index("seq")
    group = lax.axis_index("mp")
    rows = qkv_ref.shape[1]
    slots = rows * mps // seqs
    own_slots = rows // slots
    heads = qkv_ref.shape[2] // HEAD
    mine = heads // mps
    part = slots // SPLIT

    def load(head):
        return pltpu.make_async_copy(
            qkv_ref.at[:, :, pl.ds(pl.multiple_of(head * HEAD, HEAD), HEAD)],
            qkv_v.at[head],
            load_sem.at[head],
        )

    def start_loads(step, carry):
        peer = (group + 1 + step % mps) % mps
        load(peer * mine + step // mps).start()
        return carry

    lax.fori_loop(0, heads, start_loads, 0)

    barrier = pltpu.get_barrier_semaphore()

    def greet_mp(step, carry):
        pl.semaphore_signal(
            barrier, inc=1, device_id=(me, (group + 1 + step) % mps), device_id_type=MESH
        )
        return carry

    def greet_seq(step, carry):
        pl.semaphore_signal(
            barrier, inc=1, device_id=((me + 1 + step) % seqs, group), device_id_type=MESH
        )
        return carry

    lax.fori_loop(0, mps - 1, greet_mp, 0)
    lax.fori_loop(0, seqs - 1, greet_seq, 0)

    lane = lax.broadcasted_iota(jnp.int32, (1, 128), 1)
    slot_of = jnp.zeros((1, 128), jnp.int32)
    for i in range(seqs):
        slot_of = jnp.where(lane == offset_ref[i], i, slot_of)
    slot_v[...] = slot_of
    slot_copy = pltpu.make_async_copy(slot_v, slot_s, slot_sem)
    slot_copy.start()

    row = lax.broadcasted_iota(jnp.int32, (rows, rows), 0)
    column = lax.broadcasted_iota(jnp.int32, (rows, rows), 1)
    meet = row // (slots // 2) == column // (slots // 2)
    for a in range(own_slots):
        slot = own_slots * group + a
        pack = (me - offset_ref[slot] + seqs) % seqs
        same = jnp.where(segment_ref[pack, 2 * slot] == segment_ref[pack, 2 * slot + 1], 1, 0)
        inside = (row // slots == a) & (column // slots == a)
        meet = meet | (inside & (jnp.full((rows, rows), same, jnp.int32) == 1))
    bias = jnp.where(meet, 0.0, -1e30)

    def attend(head):
        q, k, v = qkv_v[head, 0], qkv_v[head, 1], qkv_v[head, 2]
        scores = lax.dot_general(
            q, k, (((1,), (1,)), ((), ())), preferred_element_type=jnp.float32
        )
        scores = scores * (LOG2E / math.sqrt(HEAD)) + bias
        exponent = jnp.exp2(scores - jnp.max(scores, axis=-1, keepdims=True))
        weights = exponent / jnp.sum(exponent, axis=-1, keepdims=True)
        return jnp.dot(
            weights.astype(jnp.bfloat16), v, preferred_element_type=jnp.float32
        ).astype(jnp.bfloat16)

    def first_start(half, r, peer):
        c = half * SPLIT + r
        block = first_in[c].at[pl.ds(own_slots * group, own_slots)]

        @pl.when(peer != group)
        def _():
            pltpu.make_async_remote_copy(
                first_out.at[c, peer], block, first_send.at[c], first_recv.at[c],
                device_id=(me, peer), device_id_type=MESH,
            ).start()

        @pl.when(peer == group)
        def _():
            pltpu.make_async_copy(first_out.at[c, peer], block, first_recv.at[c]).start()

    def compute(half):
        def some_heads(step, carry):
            peers = [(group + 1 + step * UNROLL + u) % mps for u in range(UNROLL)]
            for peer in peers:
                load(peer * mine + half).wait()
            values = [attend(peer * mine + half) for peer in peers]
            for peer, value in zip(peers, values):
                value = value.reshape(own_slots, slots, HEAD)
                for r in range(SPLIT):
                    first_out[half * SPLIT + r, peer] = value[:, r * part:(r + 1) * part]
            for peer in peers:
                first_start(half, 0, peer)
            return carry

        def rest(r, step, carry):
            first_start(half, r, (group + 1 + step) % mps)
            return carry

        lax.fori_loop(0, mps // UNROLL, some_heads, 0)
        for r in range(1, SPLIT):
            lax.fori_loop(0, mps, functools.partial(rest, r), 0)

    def forward(c):
        pltpu.make_async_copy(first_in[c], first_in[c], first_recv.at[c]).wait()

        def send(step, carry):
            pack = ring_peer(me, step, seqs)
            slot = slot_s[0, (me - pack + seqs) % seqs]
            second_out[c, pack] = first_in[c][slot]
            pltpu.make_async_remote_copy(
                second_out.at[c, pack], second_in[c].at[me], second_send.at[c], second_recv.at[c],
                device_id=(pack, group), device_id_type=MESH,
            ).start()
            return carry

        lax.fori_loop(0, seqs - 1, send, 0)
        second_in[c][me] = first_in[c][slot_s[0, 0]]

    def finish(c):
        half, r = c // SPLIT, c % SPLIT
        landed = second_in[c].at[pl.ds(0, seqs - 1)]
        pltpu.make_async_copy(landed, landed, second_recv.at[c]).wait()

        def place(slot, carry):
            loader = (me + offset_ref[slot]) % seqs
            result[slot, r * part:(r + 1) * part, half * HEAD:(half + 1) * HEAD] = second_in[c][loader]
            return carry

        lax.fori_loop(0, seqs, place, 0)
        store(c).start()

    def store(c):
        half, r = c // SPLIT, c % SPLIT
        where = (slice(None), pl.ds(r * part, part), pl.ds(half * HEAD, HEAD))
        return pltpu.make_async_copy(result.at[where], out_ref.at[where], out_sem.at[c])

    chunks = mine * SPLIT
    pl.semaphore_wait(barrier, mps - 1 + seqs - 1)
    compute(0)
    slot_copy.wait()
    forward(0)
    for half in range(1, mine):
        compute(half)
    for c in range(1, chunks):
        forward(c)
        if c >= 2:
            finish(c - 2)
    for c in range(max(chunks - 2, 0), chunks):
        finish(c)
    for c in range(chunks):
        sent = first_out.at[c, pl.ds(0, mps - 1)]
        pltpu.make_async_copy(sent, sent, first_send.at[c]).wait()
        sent = second_out.at[c, pl.ds(0, seqs - 1)]
        pltpu.make_async_copy(sent, sent, second_send.at[c]).wait()
        store(c).wait()


def on_device(seqs, mps, qkv, pack_segments, slot_offset):
    members, rows, features = qkv.shape
    heads = features // HEAD
    mine = heads // mps
    slots = rows * mps // seqs
    own_slots = rows // slots
    part = slots // SPLIT
    chunks = mine * SPLIT
    smem = pl.BlockSpec(memory_space=pltpu.SMEM)
    out = pl.pallas_call(
        functools.partial(kernel, seqs, mps),
        out_shape=jax.ShapeDtypeStruct((seqs, slots, mine * HEAD), jnp.bfloat16),
        in_specs=[smem, smem, pl.BlockSpec(memory_space=pl.ANY)],
        out_specs=pl.BlockSpec(memory_space=pl.ANY),
        scratch_shapes=[
            pltpu.VMEM((heads, members, rows, HEAD), jnp.bfloat16),
            pltpu.VMEM((chunks, mps, own_slots, part, HEAD), jnp.bfloat16),
            pltpu.VMEM((chunks, seqs, part, HEAD), jnp.bfloat16),
            pltpu.VMEM((seqs, slots, mine * HEAD), jnp.bfloat16),
            pltpu.VMEM((1, 128), jnp.int32),
            pltpu.SMEM((1, 128), jnp.int32),
            pltpu.SemaphoreType.DMA((heads,)),
            pltpu.SemaphoreType.DMA,
            pltpu.SemaphoreType.DMA((chunks,)),
            pltpu.SemaphoreType.DMA((chunks,)),
            pltpu.SemaphoreType.DMA((chunks,)),
            pltpu.SemaphoreType.DMA((chunks,)),
            pltpu.SemaphoreType.DMA((chunks,)),
        ] + [pltpu.VMEM((seqs, part, HEAD), jnp.bfloat16)] * (2 * chunks),
        compiler_params=pltpu.CompilerParams(
            collective_id=0, has_side_effects=True, vmem_limit_bytes=32 * 1024 * 1024
        ),
        cost_estimate=pl.CostEstimate(
            flops=4 * heads * rows * rows * HEAD,
            bytes_accessed=2 * (members + 1) * rows * features,
            transcendentals=heads * rows * rows,
        ),
    )(slot_offset, pack_segments, qkv)
    return out.reshape(seqs * slots, mine * HEAD)


def solution(mesh):
    return jax.shard_map(
        functools.partial(on_device, mesh.shape["seq"], mesh.shape["mp"]),
        mesh=mesh,
        in_specs=(P(None, ("seq", "mp"), None), P(), P()),
        out_specs=P("seq", "mp"),
        check_vma=False,
    )
```

```python
import functools
import math

import jax
import jax.numpy as jnp
from jax import lax
from jax.experimental import pallas as pl
from jax.experimental.pallas import tpu as pltpu
from jax.sharding import PartitionSpec as P

HEAD = 128
LOG2E = 1.4426950408889634
MESH = pl.DeviceIdType.MESH
SPLIT = 2
UNROLL = 8


def ring_peer(own, step, count):
    chips = count // 2
    k = step // 2
    away = chips // 2 - (k + 1) // 2
    turn = jnp.where(k % 2 == 1, away, chips - away)
    chip = (own // 2 + turn) % chips
    return 2 * chip + (own + step + 1) % 2


def kernel(
    seqs, mps, offset_hbm, segment_hbm, qkv_ref, out_ref,
    qkv_v, first_out, second_out, offset_ref, segment_ref, slot_v, slot_s,
    load_sem, index_sem, first_send, first_recv, second_send, second_recv, word, *landing,
):
    first_in, second_in = landing[:len(landing) // 2], landing[len(landing) // 2:]
    me = lax.axis_index("seq")
    group = lax.axis_index("mp")
    rows = qkv_ref.shape[1]
    slots = rows * mps // seqs
    own_slots = rows // slots
    heads = qkv_ref.shape[2] // HEAD
    mine = heads // mps
    part = slots // SPLIT

    def load(head):
        return pltpu.make_async_copy(
            qkv_ref.at[:, :, pl.ds(pl.multiple_of(head * HEAD, HEAD), HEAD)],
            qkv_v.at[head],
            load_sem.at[head],
        )

    def start_loads(step, carry):
        peer = (group + 1 + step % mps) % mps
        load(peer * mine + step // mps).start()
        return carry

    offset_copy = pltpu.make_async_copy(offset_hbm, offset_ref, index_sem.at[0])
    segment_copy = pltpu.make_async_copy(segment_hbm, segment_ref, index_sem.at[1])
    offset_copy.start()
    segment_copy.start()
    lax.fori_loop(0, heads, start_loads, 0)

    core = me % 2
    barrier = pltpu.get_barrier_semaphore()
    sibling = (me + 1 - 2 * core, group)
    plane_others, ring_others = mps - 1, seqs // 2 - 1

    def greet_plane(step, carry):
        other = (me - core, (group + 1 + step) % mps)
        pl.semaphore_signal(barrier, inc=1, device_id=other, device_id_type=MESH)
        return carry

    def greet_ring(step, carry):
        other = ((me - core + 2 * (1 + step)) % seqs + 1, group)
        pl.semaphore_signal(barrier, inc=1, device_id=other, device_id_type=MESH)
        return carry

    pl.semaphore_signal(barrier, inc=1, device_id=sibling, device_id_type=MESH)
    lax.fori_loop(0, plane_others, greet_plane, 0)
    lax.fori_loop(0, ring_others, greet_ring, 0)

    def wait_plane():
        @pl.when(core == 0)
        def _():
            pl.semaphore_wait(barrier, 2 * plane_others + 1)
            pl.semaphore_signal(word, inc=1, device_id=sibling, device_id_type=MESH)

        @pl.when(core == 1)
        def _():
            pl.semaphore_wait(word, 1)

    def wait_ring():
        @pl.when(core == 0)
        def _():
            pl.semaphore_wait(word, 1)

        @pl.when(core == 1)
        def _():
            pl.semaphore_wait(barrier, 2 * ring_others + 1)
            pl.semaphore_signal(word, inc=1, device_id=sibling, device_id_type=MESH)

    offset_copy.wait()
    segment_copy.wait()

    lane = lax.broadcasted_iota(jnp.int32, (1, 128), 1)
    slot_of = jnp.zeros((1, 128), jnp.int32)
    for i in range(seqs):
        slot_of = jnp.where(lane == offset_ref[i], i, slot_of)
    slot_v[...] = slot_of
    slot_copy = pltpu.make_async_copy(slot_v, slot_s, index_sem.at[2])
    slot_copy.start()

    key = lax.broadcasted_iota(jnp.int32, (slots, rows), 0)
    query = lax.broadcasted_iota(jnp.int32, (slots, rows), 1)
    block = slots // 2
    meet = key // block == query % slots // block
    for a in range(own_slots):
        slot = own_slots * group + a
        pack = (me - offset_ref[slot] + seqs) % seqs
        same = jnp.where(segment_ref[pack, 2 * slot] == segment_ref[pack, 2 * slot + 1], 1, 0)
        meet = meet | ((query // slots == a) & (jnp.full((slots, rows), same, jnp.int32) == 1))
    bias = jnp.where(meet, 0.0, -1e30)
    own = [query // slots == a for a in range(own_slots)]
    diagonal = lax.broadcasted_iota(jnp.int32, (rows, rows), 0) == lax.broadcasted_iota(jnp.int32, (rows, rows), 1)
    identity = jnp.where(diagonal, 1.0, 0.0).astype(jnp.bfloat16)

    def attend(some):
        across = (((1,), (1,)), ((), ()))
        every = [
            lax.dot_general(qkv_v[h, 1], qkv_v[h, 0], across, preferred_element_type=jnp.float32) for h in some
        ]
        scores = []
        for x in every:
            mixed = x[:slots]
            for a in range(1, own_slots):
                mixed = jnp.where(own[a], x[a * slots:(a + 1) * slots], mixed)
            scores.append(mixed * (LOG2E / math.sqrt(HEAD)) + bias)
        peaks = [jnp.max(x, axis=0, keepdims=True) for x in scores]
        exponents = [jnp.exp2(x - peak) for x, peak in zip(scores, peaks)]
        totals = [1.0 / jnp.sum(x, axis=0, keepdims=True) for x in exponents]
        weights = [x * total for x, total in zip(exponents, totals)]
        weights = [
            jnp.concatenate([jnp.where(mask, x, 0.0) for mask in own], axis=0).astype(jnp.bfloat16) for x in weights
        ]
        turned = [
            lax.dot_general(identity, x, across, preferred_element_type=jnp.float32).astype(jnp.bfloat16)
            for x in weights
        ]
        return [
            jnp.dot(x, qkv_v[h, 2], preferred_element_type=jnp.float32).astype(jnp.bfloat16)
            for x, h in zip(turned, some)
        ]

    def first_start(c, peer):
        block = first_in[c].at[pl.ds(own_slots * group, own_slots)]

        @pl.when(peer != group)
        def _():
            pltpu.make_async_remote_copy(
                first_out.at[c, peer], block, first_send.at[c], first_recv.at[c],
                device_id=(me, peer), device_id_type=MESH,
            ).start()

        @pl.when(peer == group)
        def _():
            pltpu.make_async_copy(first_out.at[c, peer], block, first_recv.at[c]).start()

    def compute(half):
        def some_heads(step, carry):
            peers = [(group + 1 + step * UNROLL + u) % mps for u in range(UNROLL)]
            for peer in peers:
                load(peer * mine + half).wait()
            values = attend([peer * mine + half for peer in peers])
            for peer, value in zip(peers, values):
                value = value.reshape(own_slots, slots, HEAD)
                for r in range(SPLIT):
                    first_out[half * SPLIT + r, peer] = value[:, r * part:(r + 1) * part]
            return carry

        lax.fori_loop(0, mps // UNROLL, some_heads, 0)

    def spread(c):
        def one(step, carry):
            first_start(c, (group + 1 + step) % mps)
            return carry

        lax.fori_loop(0, mps, one, 0)

    def forward(c):
        def send(step, carry):
            pack = ring_peer(me, step, seqs)
            slot = slot_s[0, (me - pack + seqs) % seqs]
            second_out[c, pack] = first_in[c][slot]
            pltpu.make_async_remote_copy(
                second_out.at[c, pack], second_in[c].at[me], second_send.at[c], second_recv.at[c],
                device_id=(pack, group), device_id_type=MESH,
            ).start()
            return carry

        lax.fori_loop(0, seqs - 1, send, 0)
        second_in[c][me] = first_in[c][slot_s[0, 0]]

    def finish(c):
        half, r = c // SPLIT, c % SPLIT
        landed = second_in[c].at[pl.ds(0, seqs - 1)]
        pltpu.make_async_copy(landed, landed, second_recv.at[c]).wait()

        def place(slot, carry):
            loader = (me + offset_ref[slot]) % seqs
            out_ref[slot, r * part:(r + 1) * part, half * HEAD:(half + 1) * HEAD] = second_in[c][loader]
            return carry

        lax.fori_loop(0, seqs, place, 0)

    chunks = mine * SPLIT
    compute(0)
    wait_plane()
    for c in range(SPLIT):
        spread(c)
    slot_copy.wait()
    for c in range(chunks):
        pltpu.make_async_copy(first_in[c], first_in[c], first_recv.at[c]).wait()
        if c == 0:
            wait_ring()
        forward(c)
        if (c + 1) % SPLIT == 0 and c + 1 < chunks:
            compute((c + 1) // SPLIT)
            for other in range(c + 1, c + 1 + SPLIT):
                spread(other)
    for c in range(chunks):
        finish(c)
    for c in range(chunks):
        sent = first_out.at[c, pl.ds(0, mps - 1)]
        pltpu.make_async_copy(sent, sent, first_send.at[c]).wait()
        sent = second_out.at[c, pl.ds(0, seqs - 1)]
        pltpu.make_async_copy(sent, sent, second_send.at[c]).wait()


def on_device(seqs, mps, qkv, pack_segments, slot_offset):
    members, rows, features = qkv.shape
    heads = features // HEAD
    mine = heads // mps
    slots = rows * mps // seqs
    own_slots = rows // slots
    part = slots // SPLIT
    chunks = mine * SPLIT
    hbm = pl.BlockSpec(memory_space=pltpu.HBM)
    out = pl.pallas_call(
        functools.partial(kernel, seqs, mps),
        out_shape=jax.ShapeDtypeStruct((seqs, slots, mine * HEAD), jnp.bfloat16),
        in_specs=[hbm, hbm, hbm],
        out_specs=pl.BlockSpec(memory_space=pltpu.VMEM),
        scratch_shapes=[
            pltpu.VMEM((heads, members, rows, HEAD), jnp.bfloat16),
            pltpu.VMEM((chunks, mps, own_slots, part, HEAD), jnp.bfloat16),
            pltpu.VMEM((chunks, seqs, part, HEAD), jnp.bfloat16),
            pltpu.SMEM(slot_offset.shape, jnp.int32),
            pltpu.SMEM(pack_segments.shape, jnp.int32),
            pltpu.VMEM((1, 128), jnp.int32),
            pltpu.SMEM((1, 128), jnp.int32),
            pltpu.SemaphoreType.DMA((heads,)),
            pltpu.SemaphoreType.DMA((3,)),
            pltpu.SemaphoreType.DMA((chunks,)),
            pltpu.SemaphoreType.DMA((chunks,)),
            pltpu.SemaphoreType.DMA((chunks,)),
            pltpu.SemaphoreType.DMA((chunks,)),
            pltpu.SemaphoreType.REGULAR,
        ] + [pltpu.VMEM((seqs, part, HEAD), jnp.bfloat16)] * (2 * chunks),
        compiler_params=pltpu.CompilerParams(
            collective_id=0, has_side_effects=True, vmem_limit_bytes=32 * 1024 * 1024
        ),
        cost_estimate=pl.CostEstimate(
            flops=4 * heads * rows * rows * HEAD,
            bytes_accessed=2 * (members + 1) * rows * features,
            transcendentals=heads * rows * rows,
        ),
    )(*(pltpu.with_memory_space_constraint(x, pltpu.HBM) for x in (slot_offset, pack_segments, qkv)))
    return out.reshape(seqs * slots, mine * HEAD)


def solution(mesh):
    return jax.shard_map(
        functools.partial(on_device, mesh.shape["seq"], mesh.shape["mp"]),
        mesh=mesh,
        in_specs=(P(None, ("seq", "mp"), None), P(), P()),
        out_specs=P("seq", "mp"),
        check_vma=False,
    )
```

```python
import functools
import math

import jax
import jax.numpy as jnp
from jax import lax
from jax.experimental import pallas as pl
from jax.experimental.pallas import tpu as pltpu
from jax.sharding import PartitionSpec as P

HEAD = 128
AHEAD = 2
LOG2E = 1.4426950408889634
MESH = pl.DeviceIdType.MESH
CHUNKS = ((0, 0, 16), (0, 16, 32), (0, 32, 64), (1, 0, 64))
UNROLL = 8


def ring_peer(own, step, count):
    chips = count // 2
    k = step // 2
    away = chips // 2 - (k + 1) // 2
    turn = jnp.where(k % 2 == 1, away, chips - away)
    chip = (own // 2 + turn) % chips
    return 2 * chip + (own + step + 1) % 2


def kernel(
    seqs, mps, offset_hbm, segment_hbm, qkv_ref, out_ref,
    qkv_v, offset_ref, segment_ref, slot_v, slot_s,
    load_sem, index_sem, first_send, first_recv, second_send, second_recv, word, *landing,
):
    chunks = len(CHUNKS)
    first_out, first_in, second_out, second_in = (landing[i * chunks:(i + 1) * chunks] for i in range(4))
    me = lax.axis_index("seq")
    group = lax.axis_index("mp")
    rows = qkv_ref.shape[1]
    slots = rows * mps // seqs
    own_slots = rows // slots
    heads = qkv_ref.shape[2] // HEAD
    mine = heads // mps

    def load(head):
        return pltpu.make_async_copy(
            qkv_ref.at[:, :, pl.ds(pl.multiple_of(head * HEAD, HEAD), HEAD)],
            qkv_v.at[head],
            load_sem.at[head],
        )

    def start_loads(step, carry):
        peer = (group + 1 + step % mps) % mps
        load(peer * mine + step // mps).start()
        return carry

    offset_copy = pltpu.make_async_copy(offset_hbm, offset_ref, index_sem.at[0])
    segment_copy = pltpu.make_async_copy(segment_hbm, segment_ref, index_sem.at[1])
    offset_copy.start()
    segment_copy.start()
    lax.fori_loop(0, heads, start_loads, 0)

    core = me % 2
    barrier = pltpu.get_barrier_semaphore()
    sibling = (me + 1 - 2 * core, group)
    plane_others, ring_others = mps - 1, seqs // 2 - 1

    def greet_plane(step, carry):
        other = (me - core, (group + 1 + step) % mps)
        pl.semaphore_signal(barrier, inc=1, device_id=other, device_id_type=MESH)
        return carry

    def greet_ring(step, carry):
        other = ((me - core + 2 * (1 + step)) % seqs + 1, group)
        pl.semaphore_signal(barrier, inc=1, device_id=other, device_id_type=MESH)
        return carry

    pl.semaphore_signal(barrier, inc=1, device_id=sibling, device_id_type=MESH)
    lax.fori_loop(0, plane_others, greet_plane, 0)
    lax.fori_loop(0, ring_others, greet_ring, 0)

    def wait_plane():
        @pl.when(core == 0)
        def _():
            pl.semaphore_wait(barrier, 2 * plane_others + 1)
            pl.semaphore_signal(word, inc=1, device_id=sibling, device_id_type=MESH)

        @pl.when(core == 1)
        def _():
            pl.semaphore_wait(word, 1)

    def wait_ring():
        @pl.when(core == 0)
        def _():
            pl.semaphore_wait(word, 1)

        @pl.when(core == 1)
        def _():
            pl.semaphore_wait(barrier, 2 * ring_others + 1)
            pl.semaphore_signal(word, inc=1, device_id=sibling, device_id_type=MESH)

    offset_copy.wait()
    segment_copy.wait()

    lane = lax.broadcasted_iota(jnp.int32, (1, 128), 1)
    slot_of = jnp.zeros((1, 128), jnp.int32)
    for i in range(seqs):
        slot_of = jnp.where(lane == offset_ref[i], i, slot_of)
    slot_v[...] = slot_of
    slot_copy = pltpu.make_async_copy(slot_v, slot_s, index_sem.at[2])
    slot_copy.start()

    key = lax.broadcasted_iota(jnp.int32, (slots, rows), 0)
    query = lax.broadcasted_iota(jnp.int32, (slots, rows), 1)
    block = slots // 2
    meet = key // block == query % slots // block
    for a in range(own_slots):
        slot = own_slots * group + a
        pack = (me - offset_ref[slot] + seqs) % seqs
        same = jnp.where(segment_ref[pack, 2 * slot] == segment_ref[pack, 2 * slot + 1], 1, 0)
        meet = meet | ((query // slots == a) & (jnp.full((slots, rows), same, jnp.int32) == 1))
    bias = jnp.where(meet, 0.0, -1e30)
    own = [query // slots == a for a in range(own_slots)]
    diagonal = lax.broadcasted_iota(jnp.int32, (rows, rows), 0) == lax.broadcasted_iota(jnp.int32, (rows, rows), 1)
    identity = jnp.where(diagonal, 1.0, 0.0).astype(jnp.bfloat16)

    def attend(some):
        across = (((1,), (1,)), ((), ()))
        every = [
            lax.dot_general(qkv_v[h, 1], qkv_v[h, 0], across, preferred_element_type=jnp.float32) for h in some
        ]
        scores = []
        for x in every:
            mixed = x[:slots]
            for a in range(1, own_slots):
                mixed = jnp.where(own[a], x[a * slots:(a + 1) * slots], mixed)
            scores.append(mixed * (LOG2E / math.sqrt(HEAD)) + bias)
        peaks = [jnp.max(x, axis=0, keepdims=True) for x in scores]
        exponents = [jnp.exp2(x - peak) for x, peak in zip(scores, peaks)]
        totals = [1.0 / jnp.sum(x, axis=0, keepdims=True) for x in exponents]
        weights = [x * total for x, total in zip(exponents, totals)]
        weights = [
            jnp.concatenate([jnp.where(mask, x, 0.0) for mask in own], axis=0).astype(jnp.bfloat16) for x in weights
        ]
        turned = [
            lax.dot_general(identity, x, across, preferred_element_type=jnp.float32).astype(jnp.bfloat16)
            for x in weights
        ]
        return [
            jnp.dot(x, qkv_v[h, 2], preferred_element_type=jnp.float32).astype(jnp.bfloat16)
            for x, h in zip(turned, some)
        ]

    def first_start(c, peer):
        block = first_in[c].at[pl.ds(own_slots * group, own_slots)]

        @pl.when(peer != group)
        def _():
            pltpu.make_async_remote_copy(
                first_out[c].at[peer], block, first_send.at[c], first_recv.at[c],
                device_id=(me, peer), device_id_type=MESH,
            ).start()

        @pl.when(peer == group)
        def _():
            pltpu.make_async_copy(first_out[c].at[peer], block, first_recv.at[c]).start()

    def compute(half):
        def some_heads(step, carry):
            peers = [(group + 1 + step * UNROLL + u) % mps for u in range(UNROLL)]
            for peer in peers:
                load(peer * mine + half).wait()
            values = attend([peer * mine + half for peer in peers])
            for peer, value in zip(peers, values):
                value = value.reshape(own_slots, slots, HEAD)
                for c, (head, start, stop) in enumerate(CHUNKS):
                    if head == half:
                        first_out[c][peer] = value[:, start:stop]
            return carry

        lax.fori_loop(0, mps // UNROLL, some_heads, 0)

    def spread(c):
        def one(step, carry):
            first_start(c, (group + 1 + step) % mps)
            return carry

        lax.fori_loop(0, mps, one, 0, unroll=4)

    def forward(c):
        def send(step, carry):
            pack = ring_peer(me, step, seqs)
            slot = slot_s[0, (me - pack + seqs) % seqs]
            second_out[c][pack] = first_in[c][slot]
            pltpu.make_async_remote_copy(
                second_out[c].at[pack], second_in[c].at[me], second_send.at[c], second_recv.at[c],
                device_id=(pack, group), device_id_type=MESH,
            ).start()
            return carry

        lax.fori_loop(0, seqs - 1, send, 0, unroll=31)
        second_in[c][me] = first_in[c][slot_s[0, 0]]

    def finish(c):
        half, start, stop = CHUNKS[c]
        landed = second_in[c].at[pl.ds(0, seqs - 1)]
        pltpu.make_async_copy(landed, landed, second_recv.at[c]).wait()

        def place(slot, carry):
            loader = (me + offset_ref[slot]) % seqs
            out_ref[slot, start:stop, half * HEAD:(half + 1) * HEAD] = second_in[c][loader]
            return carry

        lax.fori_loop(0, seqs, place, 0, unroll=8)

    compute(0)
    wait_plane()
    for c in range(AHEAD):
        spread(c)
    slot_copy.wait()
    wait_ring()
    for c in range(chunks):
        if CHUNKS[c][0] > 0 and CHUNKS[c][1] == 0:
            compute(CHUNKS[c][0])
            for other in range(c, chunks):
                if CHUNKS[other][0] == CHUNKS[c][0]:
                    spread(other)
        pltpu.make_async_copy(first_in[c], first_in[c], first_recv.at[c]).wait()
        if c + AHEAD < chunks and CHUNKS[c + AHEAD][0] == 0:
            spread(c + AHEAD)
        forward(c)
    for c in range(chunks):
        finish(c)
    for c in range(chunks):
        sent = first_out[c].at[pl.ds(0, mps - 1)]
        pltpu.make_async_copy(sent, sent, first_send.at[c]).wait()
        sent = second_out[c].at[pl.ds(0, seqs - 1)]
        pltpu.make_async_copy(sent, sent, second_send.at[c]).wait()


def on_device(seqs, mps, qkv, pack_segments, slot_offset):
    members, rows, features = qkv.shape
    heads = features // HEAD
    mine = heads // mps
    slots = rows * mps // seqs
    own_slots = rows // slots
    chunks = len(CHUNKS)
    parts = [stop - start for _, start, stop in CHUNKS]
    by_loader = [pltpu.VMEM((seqs, part, HEAD), jnp.bfloat16) for part in parts]
    by_group = [pltpu.VMEM((mps, own_slots, part, HEAD), jnp.bfloat16) for part in parts]
    hbm = pl.BlockSpec(memory_space=pltpu.HBM)
    out = pl.pallas_call(
        functools.partial(kernel, seqs, mps),
        out_shape=jax.ShapeDtypeStruct((seqs, slots, mine * HEAD), jnp.bfloat16),
        in_specs=[hbm, hbm, hbm],
        out_specs=pl.BlockSpec(memory_space=pltpu.VMEM),
        scratch_shapes=[
            pltpu.VMEM((heads, members, rows, HEAD), jnp.bfloat16),
            pltpu.SMEM(slot_offset.shape, jnp.int32),
            pltpu.SMEM(pack_segments.shape, jnp.int32),
            pltpu.VMEM((1, 128), jnp.int32),
            pltpu.SMEM((1, 128), jnp.int32),
            pltpu.SemaphoreType.DMA((heads,)),
            pltpu.SemaphoreType.DMA((3,)),
            pltpu.SemaphoreType.DMA((chunks,)),
            pltpu.SemaphoreType.DMA((chunks,)),
            pltpu.SemaphoreType.DMA((chunks,)),
            pltpu.SemaphoreType.DMA((chunks,)),
            pltpu.SemaphoreType.REGULAR,
        ] + by_group + 3 * by_loader,
        compiler_params=pltpu.CompilerParams(
            collective_id=0, has_side_effects=True, vmem_limit_bytes=32 * 1024 * 1024
        ),
        cost_estimate=pl.CostEstimate(
            flops=4 * heads * rows * rows * HEAD,
            bytes_accessed=2 * (members + 1) * rows * features,
            transcendentals=heads * rows * rows,
        ),
    )(*(pltpu.with_memory_space_constraint(x, pltpu.HBM) for x in (slot_offset, pack_segments, qkv)))
    return out.reshape(seqs * slots, mine * HEAD)


def solution(mesh):
    return jax.shard_map(
        functools.partial(on_device, mesh.shape["seq"], mesh.shape["mp"]),
        mesh=mesh,
        in_specs=(P(None, ("seq", "mp"), None), P(), P()),
        out_specs=P("seq", "mp"),
        check_vma=False,
    )
```

```python
import functools
import math

import jax
import jax.numpy as jnp
from jax import lax
from jax.experimental import pallas as pl
from jax.experimental.pallas import tpu as pltpu
from jax.sharding import PartitionSpec as P

HEAD = 128
AHEAD = 2
LOG2E = 1.4426950408889634
MESH = pl.DeviceIdType.MESH
CHUNKS = ((0, 0, 16), (0, 16, 32), (0, 32, 64), (1, 0, 64))
UNROLL = 8


def ring_peer(own, step, count):
    chips = count // 2
    k = step // 2
    away = chips // 2 - (k + 1) // 2
    turn = jnp.where(k % 2 == 1, away, chips - away)
    chip = (own // 2 + turn) % chips
    return 2 * chip + (own + step + 1) % 2


def kernel(
    seqs, mps, offset_hbm, segment_hbm, qkv_ref, out_ref,
    qkv_v, offset_ref, segment_ref, slot_v, slot_s,
    load_sem, index_sem, first_send, first_recv, second_send, second_recv, word, *landing,
):
    chunks = len(CHUNKS)
    first_out, first_in, second_out, second_in = (landing[i * chunks:(i + 1) * chunks] for i in range(4))
    me = lax.axis_index("seq")
    group = lax.axis_index("mp")
    rows = qkv_ref.shape[1]
    slots = rows * mps // seqs
    own_slots = rows // slots
    heads = qkv_ref.shape[2] // HEAD
    mine = heads // mps

    def load(head):
        return pltpu.make_async_copy(
            qkv_ref.at[:, :, pl.ds(pl.multiple_of(head * HEAD, HEAD), HEAD)],
            qkv_v.at[head],
            load_sem.at[head],
        )

    def start_loads(step, carry):
        peer = (group + 1 + step % mps) % mps
        load(peer * mine + step // mps).start()
        return carry

    offset_copy = pltpu.make_async_copy(offset_hbm, offset_ref, index_sem.at[0])
    segment_copy = pltpu.make_async_copy(segment_hbm, segment_ref, index_sem.at[1])
    offset_copy.start()
    segment_copy.start()

    core = me % 2
    barrier = pltpu.get_barrier_semaphore()
    sibling = (me + 1 - 2 * core, group)
    plane_others, ring_others = mps - 1, seqs // 2 - 1

    def greet_plane(step, carry):
        other = (me - core, (group + 1 + step) % mps)
        pl.semaphore_signal(barrier, inc=1, device_id=other, device_id_type=MESH)
        return carry

    def greet_ring(step, carry):
        other = ((me - core + 2 * (1 + step)) % seqs + 1, group)
        pl.semaphore_signal(barrier, inc=1, device_id=other, device_id_type=MESH)
        return carry

    pl.semaphore_signal(barrier, inc=1, device_id=sibling, device_id_type=MESH)
    lax.fori_loop(0, plane_others, greet_plane, 0, unroll=5)
    lax.fori_loop(0, mps, start_loads, 0, unroll=4)
    lax.fori_loop(0, ring_others, greet_ring, 0, unroll=5)
    lax.fori_loop(mps, heads, start_loads, 0, unroll=4)

    def wait_plane():
        @pl.when(core == 0)
        def _():
            pl.semaphore_wait(barrier, 2 * plane_others + 1)
            pl.semaphore_signal(word, inc=1, device_id=sibling, device_id_type=MESH)

        @pl.when(core == 1)
        def _():
            pl.semaphore_wait(word, 1)

    def wait_ring():
        @pl.when(core == 0)
        def _():
            pl.semaphore_wait(word, 1)

        @pl.when(core == 1)
        def _():
            pl.semaphore_wait(barrier, 2 * ring_others + 1)
            pl.semaphore_signal(word, inc=1, device_id=sibling, device_id_type=MESH)

    offset_copy.wait()
    segment_copy.wait()

    lane = lax.broadcasted_iota(jnp.int32, (1, 128), 1)
    slot_of = jnp.zeros((1, 128), jnp.int32)
    for i in range(seqs):
        slot_of = jnp.where(lane == offset_ref[i], i, slot_of)
    slot_v[...] = slot_of
    slot_copy = pltpu.make_async_copy(slot_v, slot_s, index_sem.at[2])
    slot_copy.start()

    key = lax.broadcasted_iota(jnp.int32, (slots, rows), 0)
    query = lax.broadcasted_iota(jnp.int32, (slots, rows), 1)
    block = slots // 2
    meet = key // block == query % slots // block
    for a in range(own_slots):
        slot = own_slots * group + a
        pack = (me - offset_ref[slot] + seqs) % seqs
        same = jnp.where(segment_ref[pack, 2 * slot] == segment_ref[pack, 2 * slot + 1], 1, 0)
        meet = meet | ((query // slots == a) & (jnp.full((slots, rows), same, jnp.int32) == 1))
    bias = jnp.where(meet, 0.0, -1e30)
    own = [query // slots == a for a in range(own_slots)]
    diagonal = lax.broadcasted_iota(jnp.int32, (rows, rows), 0) == lax.broadcasted_iota(jnp.int32, (rows, rows), 1)
    identity = jnp.where(diagonal, 1.0, 0.0).astype(jnp.bfloat16)

    def attend(some):
        across = (((1,), (1,)), ((), ()))
        every = [
            lax.dot_general(qkv_v[h, 1], qkv_v[h, 0], across, preferred_element_type=jnp.float32) for h in some
        ]
        scores = []
        for x in every:
            mixed = x[:slots]
            for a in range(1, own_slots):
                mixed = jnp.where(own[a], x[a * slots:(a + 1) * slots], mixed)
            scores.append(mixed * (LOG2E / math.sqrt(HEAD)) + bias)
        peaks = [jnp.max(x, axis=0, keepdims=True) for x in scores]
        exponents = [jnp.exp2(x - peak) for x, peak in zip(scores, peaks)]
        totals = [1.0 / jnp.sum(x, axis=0, keepdims=True) for x in exponents]
        weights = [x * total for x, total in zip(exponents, totals)]
        weights = [
            jnp.concatenate([jnp.where(mask, x, 0.0) for mask in own], axis=0).astype(jnp.bfloat16) for x in weights
        ]
        turned = [
            lax.dot_general(identity, x, across, preferred_element_type=jnp.float32).astype(jnp.bfloat16)
            for x in weights
        ]
        return [
            jnp.dot(x, qkv_v[h, 2], preferred_element_type=jnp.float32).astype(jnp.bfloat16)
            for x, h in zip(turned, some)
        ]

    def first_start(c, peer):
        block = first_in[c].at[pl.ds(own_slots * group, own_slots)]

        @pl.when(peer != group)
        def _():
            pltpu.make_async_remote_copy(
                first_out[c].at[peer], block, first_send.at[c], first_recv.at[c],
                device_id=(me, peer), device_id_type=MESH,
            ).start()

        @pl.when(peer == group)
        def _():
            pltpu.make_async_copy(first_out[c].at[peer], block, first_recv.at[c]).start()

    def compute(half):
        def some_heads(step, carry):
            peers = [(group + 1 + step * UNROLL + u) % mps for u in range(UNROLL)]
            for peer in peers:
                load(peer * mine + half).wait()
            values = attend([peer * mine + half for peer in peers])
            for peer, value in zip(peers, values):
                value = value.reshape(own_slots, slots, HEAD)
                for c, (head, start, stop) in enumerate(CHUNKS):
                    if head == half:
                        first_out[c][peer] = value[:, start:stop]
            return carry

        lax.fori_loop(0, mps // UNROLL, some_heads, 0)

    def spread(c):
        def one(step, carry):
            first_start(c, (group + 1 + step) % mps)
            return carry

        lax.fori_loop(0, mps, one, 0, unroll=4)

    def forward(c):
        def send(step, carry):
            pack = ring_peer(me, step, seqs)
            slot = slot_s[0, (me - pack + seqs) % seqs]
            second_out[c][pack] = first_in[c][slot]
            pltpu.make_async_remote_copy(
                second_out[c].at[pack], second_in[c].at[me], second_send.at[c], second_recv.at[c],
                device_id=(pack, group), device_id_type=MESH,
            ).start()
            return carry

        lax.fori_loop(0, seqs - 1, send, 0, unroll=31)
        second_in[c][me] = first_in[c][slot_s[0, 0]]

    def finish(c):
        half, start, stop = CHUNKS[c]
        landed = second_in[c].at[pl.ds(0, seqs - 1)]
        pltpu.make_async_copy(landed, landed, second_recv.at[c]).wait()

        def place(slot, carry):
            loader = (me + offset_ref[slot]) % seqs
            out_ref[slot, start:stop, half * HEAD:(half + 1) * HEAD] = second_in[c][loader]
            return carry

        lax.fori_loop(0, seqs, place, 0, unroll=8)

    compute(0)
    wait_plane()
    for c in range(AHEAD):
        spread(c)
    slot_copy.wait()
    wait_ring()
    for c in range(chunks):
        if CHUNKS[c][0] > 0 and CHUNKS[c][1] == 0:
            compute(CHUNKS[c][0])
            for other in range(c, chunks):
                if CHUNKS[other][0] == CHUNKS[c][0]:
                    spread(other)
        pltpu.make_async_copy(first_in[c], first_in[c], first_recv.at[c]).wait()
        if c + AHEAD < chunks and CHUNKS[c + AHEAD][0] == 0:
            spread(c + AHEAD)
        forward(c)
    for c in range(chunks):
        finish(c)
    for c in range(chunks):
        sent = first_out[c].at[pl.ds(0, mps - 1)]
        pltpu.make_async_copy(sent, sent, first_send.at[c]).wait()
        sent = second_out[c].at[pl.ds(0, seqs - 1)]
        pltpu.make_async_copy(sent, sent, second_send.at[c]).wait()


def on_device(seqs, mps, qkv, pack_segments, slot_offset):
    members, rows, features = qkv.shape
    heads = features // HEAD
    mine = heads // mps
    slots = rows * mps // seqs
    own_slots = rows // slots
    chunks = len(CHUNKS)
    parts = [stop - start for _, start, stop in CHUNKS]
    by_loader = [pltpu.VMEM((seqs, part, HEAD), jnp.bfloat16) for part in parts]
    by_group = [pltpu.VMEM((mps, own_slots, part, HEAD), jnp.bfloat16) for part in parts]
    hbm = pl.BlockSpec(memory_space=pltpu.HBM)
    out = pl.pallas_call(
        functools.partial(kernel, seqs, mps),
        out_shape=jax.ShapeDtypeStruct((seqs, slots, mine * HEAD), jnp.bfloat16),
        in_specs=[hbm, hbm, hbm],
        out_specs=pl.BlockSpec(memory_space=pltpu.VMEM),
        scratch_shapes=[
            pltpu.VMEM((heads, members, rows, HEAD), jnp.bfloat16),
            pltpu.SMEM(slot_offset.shape, jnp.int32),
            pltpu.SMEM(pack_segments.shape, jnp.int32),
            pltpu.VMEM((1, 128), jnp.int32),
            pltpu.SMEM((1, 128), jnp.int32),
            pltpu.SemaphoreType.DMA((heads,)),
            pltpu.SemaphoreType.DMA((3,)),
            pltpu.SemaphoreType.DMA((chunks,)),
            pltpu.SemaphoreType.DMA((chunks,)),
            pltpu.SemaphoreType.DMA((chunks,)),
            pltpu.SemaphoreType.DMA((chunks,)),
            pltpu.SemaphoreType.REGULAR,
        ] + by_group + 3 * by_loader,
        compiler_params=pltpu.CompilerParams(
            collective_id=0, has_side_effects=True, vmem_limit_bytes=32 * 1024 * 1024
        ),
        cost_estimate=pl.CostEstimate(
            flops=4 * heads * rows * rows * HEAD,
            bytes_accessed=2 * (members + 1) * rows * features,
            transcendentals=heads * rows * rows,
        ),
    )(*(pltpu.with_memory_space_constraint(x, pltpu.HBM) for x in (slot_offset, pack_segments, qkv)))
    return out.reshape(seqs * slots, mine * HEAD)


def solution(mesh):
    return jax.shard_map(
        functools.partial(on_device, mesh.shape["seq"], mesh.shape["mp"]),
        mesh=mesh,
        in_specs=(P(None, ("seq", "mp"), None), P(), P()),
        out_specs=P("seq", "mp"),
        check_vma=False,
    )
```

```python
import functools
import math

import jax
import jax.numpy as jnp
from jax import lax
from jax.experimental import pallas as pl
from jax.experimental.pallas import tpu as pltpu
from jax.sharding import PartitionSpec as P

HEAD = 128
AHEAD = 2
LOG2E = 1.4426950408889634
MESH = pl.DeviceIdType.MESH
CHUNKS = ((0, 0, 16), (0, 16, 32), (0, 32, 64), (1, 0, 64))
UNROLL = 8


def ring_peer(own, step, count):
    chips = count // 2
    k = step // 2
    away = chips // 2 - (k + 1) // 2
    turn = jnp.where(k % 2 == 1, away, chips - away)
    chip = (own // 2 + turn) % chips
    return 2 * chip + (own + step + 1) % 2


def plane_order(count):
    side = math.isqrt(count)
    steps = [(across, down) for across in range(side) for down in range(side)]
    return sorted(steps, key=lambda step: -sum(min(way, side - way) for way in step))


def kernel(
    seqs, mps, offset_hbm, segment_hbm, qkv_ref, out_ref,
    qkv_v, offset_ref, segment_ref, slot_v, slot_s,
    load_sem, index_sem, first_send, first_recv, second_send, second_recv, word, *landing,
):
    chunks = len(CHUNKS)
    first_out, first_in, second_out, second_in = (landing[i * chunks:(i + 1) * chunks] for i in range(4))
    me = lax.axis_index("seq")
    group = lax.axis_index("mp")
    rows = qkv_ref.shape[1]
    slots = rows * mps // seqs
    own_slots = rows // slots
    heads = qkv_ref.shape[2] // HEAD
    mine = heads // mps

    def load(head):
        return pltpu.make_async_copy(
            qkv_ref.at[:, :, pl.ds(pl.multiple_of(head * HEAD, HEAD), HEAD)],
            qkv_v.at[head],
            load_sem.at[head],
        )

    def start_loads(step, carry):
        peer = (group + 1 + step % mps) % mps
        load(peer * mine + step // mps).start()
        return carry

    offset_copy = pltpu.make_async_copy(offset_hbm, offset_ref, index_sem.at[0])
    segment_copy = pltpu.make_async_copy(segment_hbm, segment_ref, index_sem.at[1])
    offset_copy.start()
    segment_copy.start()
    lax.fori_loop(0, heads, start_loads, 0)

    core = me % 2
    barrier = pltpu.get_barrier_semaphore()
    sibling = (me + 1 - 2 * core, group)
    plane_others, ring_others = mps - 1, seqs // 2 - 1

    def greet_plane(step, carry):
        other = (me - core, (group + 1 + step) % mps)
        pl.semaphore_signal(barrier, inc=1, device_id=other, device_id_type=MESH)
        return carry

    def greet_ring(step, carry):
        other = ((me - core + 2 * (1 + step)) % seqs + 1, group)
        pl.semaphore_signal(barrier, inc=1, device_id=other, device_id_type=MESH)
        return carry

    pl.semaphore_signal(barrier, inc=1, device_id=sibling, device_id_type=MESH)
    lax.fori_loop(0, plane_others, greet_plane, 0)
    lax.fori_loop(0, ring_others, greet_ring, 0)

    def wait_plane():
        @pl.when(core == 0)
        def _():
            pl.semaphore_wait(barrier, 2 * plane_others + 1)
            pl.semaphore_signal(word, inc=1, device_id=sibling, device_id_type=MESH)

        @pl.when(core == 1)
        def _():
            pl.semaphore_wait(word, 1)

    def wait_ring():
        @pl.when(core == 0)
        def _():
            pl.semaphore_wait(word, 1)

        @pl.when(core == 1)
        def _():
            pl.semaphore_wait(barrier, 2 * ring_others + 1)
            pl.semaphore_signal(word, inc=1, device_id=sibling, device_id_type=MESH)

    offset_copy.wait()
    segment_copy.wait()

    lane = lax.broadcasted_iota(jnp.int32, (1, 128), 1)
    slot_of = jnp.zeros((1, 128), jnp.int32)
    for i in range(seqs):
        slot_of = jnp.where(lane == offset_ref[i], i, slot_of)
    slot_v[...] = slot_of
    slot_copy = pltpu.make_async_copy(slot_v, slot_s, index_sem.at[2])
    slot_copy.start()

    key = lax.broadcasted_iota(jnp.int32, (slots, rows), 0)
    query = lax.broadcasted_iota(jnp.int32, (slots, rows), 1)
    block = slots // 2
    meet = key // block == query % slots // block
    for a in range(own_slots):
        slot = own_slots * group + a
        pack = (me - offset_ref[slot] + seqs) % seqs
        same = jnp.where(segment_ref[pack, 2 * slot] == segment_ref[pack, 2 * slot + 1], 1, 0)
        meet = meet | ((query // slots == a) & (jnp.full((slots, rows), same, jnp.int32) == 1))
    bias = jnp.where(meet, 0.0, -1e30)
    own = [query // slots == a for a in range(own_slots)]
    diagonal = lax.broadcasted_iota(jnp.int32, (rows, rows), 0) == lax.broadcasted_iota(jnp.int32, (rows, rows), 1)
    identity = jnp.where(diagonal, 1.0, 0.0).astype(jnp.bfloat16)

    def attend(some):
        across = (((1,), (1,)), ((), ()))
        every = [
            lax.dot_general(qkv_v[h, 1], qkv_v[h, 0], across, preferred_element_type=jnp.float32) for h in some
        ]
        scores = []
        for x in every:
            mixed = x[:slots]
            for a in range(1, own_slots):
                mixed = jnp.where(own[a], x[a * slots:(a + 1) * slots], mixed)
            scores.append(mixed * (LOG2E / math.sqrt(HEAD)) + bias)
        peaks = [jnp.max(x, axis=0, keepdims=True) for x in scores]
        exponents = [jnp.exp2(x - peak) for x, peak in zip(scores, peaks)]
        totals = [1.0 / jnp.sum(x, axis=0, keepdims=True) for x in exponents]
        weights = [x * total for x, total in zip(exponents, totals)]
        weights = [
            jnp.concatenate([jnp.where(mask, x, 0.0) for mask in own], axis=0).astype(jnp.bfloat16) for x in weights
        ]
        turned = [
            lax.dot_general(identity, x, across, preferred_element_type=jnp.float32).astype(jnp.bfloat16)
            for x in weights
        ]
        return [
            jnp.dot(x, qkv_v[h, 2], preferred_element_type=jnp.float32).astype(jnp.bfloat16)
            for x, h in zip(turned, some)
        ]

    def first_start(c, peer):
        block = first_in[c].at[pl.ds(own_slots * group, own_slots)]

        @pl.when(peer != group)
        def _():
            pltpu.make_async_remote_copy(
                first_out[c].at[peer], block, first_send.at[c], first_recv.at[c],
                device_id=(me, peer), device_id_type=MESH,
            ).start()

        @pl.when(peer == group)
        def _():
            pltpu.make_async_copy(first_out[c].at[peer], block, first_recv.at[c]).start()

    def compute(half):
        def some_heads(step, carry):
            peers = [(group + 1 + step * UNROLL + u) % mps for u in range(UNROLL)]
            for peer in peers:
                load(peer * mine + half).wait()
            values = attend([peer * mine + half for peer in peers])
            for peer, value in zip(peers, values):
                value = value.reshape(own_slots, slots, HEAD)
                for c, (head, start, stop) in enumerate(CHUNKS):
                    if head == half:
                        first_out[c][peer] = value[:, start:stop]
            return carry

        lax.fori_loop(0, mps // UNROLL, some_heads, 0)

    def spread(c):
        for across, down in plane_order(mps):
            side = math.isqrt(mps)
            first_start(c, (group // side + across) % side * side + (group + down) % side)

    def forward(c):
        def send(step, carry):
            pack = ring_peer(me, step, seqs)
            slot = slot_s[0, (me - pack + seqs) % seqs]
            second_out[c][pack] = first_in[c][slot]
            pltpu.make_async_remote_copy(
                second_out[c].at[pack], second_in[c].at[me], second_send.at[c], second_recv.at[c],
                device_id=(pack, group), device_id_type=MESH,
            ).start()
            return carry

        lax.fori_loop(0, seqs - 1, send, 0, unroll=31)
        second_in[c][me] = first_in[c][slot_s[0, 0]]

    def finish(c):
        half, start, stop = CHUNKS[c]
        landed = second_in[c].at[pl.ds(0, seqs - 1)]
        pltpu.make_async_copy(landed, landed, second_recv.at[c]).wait()

        def place(slot, carry):
            loader = (me + offset_ref[slot]) % seqs
            out_ref[slot, start:stop, half * HEAD:(half + 1) * HEAD] = second_in[c][loader]
            return carry

        lax.fori_loop(0, seqs, place, 0, unroll=8)

    compute(0)
    wait_plane()
    for c in range(AHEAD):
        spread(c)
    slot_copy.wait()
    wait_ring()
    for c in range(chunks):
        if CHUNKS[c][0] > 0 and CHUNKS[c][1] == 0:
            compute(CHUNKS[c][0])
            for other in range(c, chunks):
                if CHUNKS[other][0] == CHUNKS[c][0]:
                    spread(other)
        pltpu.make_async_copy(first_in[c], first_in[c], first_recv.at[c]).wait()
        if c + AHEAD < chunks and CHUNKS[c + AHEAD][0] == 0:
            spread(c + AHEAD)
        forward(c)
    for c in range(chunks):
        finish(c)
    for c in range(chunks):
        sent = first_out[c].at[pl.ds(0, mps - 1)]
        pltpu.make_async_copy(sent, sent, first_send.at[c]).wait()
        sent = second_out[c].at[pl.ds(0, seqs - 1)]
        pltpu.make_async_copy(sent, sent, second_send.at[c]).wait()


def on_device(seqs, mps, qkv, pack_segments, slot_offset):
    members, rows, features = qkv.shape
    heads = features // HEAD
    mine = heads // mps
    slots = rows * mps // seqs
    own_slots = rows // slots
    chunks = len(CHUNKS)
    parts = [stop - start for _, start, stop in CHUNKS]
    by_loader = [pltpu.VMEM((seqs, part, HEAD), jnp.bfloat16) for part in parts]
    by_group = [pltpu.VMEM((mps, own_slots, part, HEAD), jnp.bfloat16) for part in parts]
    hbm = pl.BlockSpec(memory_space=pltpu.HBM)
    out = pl.pallas_call(
        functools.partial(kernel, seqs, mps),
        out_shape=jax.ShapeDtypeStruct((seqs, slots, mine * HEAD), jnp.bfloat16),
        in_specs=[hbm, hbm, hbm],
        out_specs=pl.BlockSpec(memory_space=pltpu.VMEM),
        scratch_shapes=[
            pltpu.VMEM((heads, members, rows, HEAD), jnp.bfloat16),
            pltpu.SMEM(slot_offset.shape, jnp.int32),
            pltpu.SMEM(pack_segments.shape, jnp.int32),
            pltpu.VMEM((1, 128), jnp.int32),
            pltpu.SMEM((1, 128), jnp.int32),
            pltpu.SemaphoreType.DMA((heads,)),
            pltpu.SemaphoreType.DMA((3,)),
            pltpu.SemaphoreType.DMA((chunks,)),
            pltpu.SemaphoreType.DMA((chunks,)),
            pltpu.SemaphoreType.DMA((chunks,)),
            pltpu.SemaphoreType.DMA((chunks,)),
            pltpu.SemaphoreType.REGULAR,
        ] + by_group + 3 * by_loader,
        compiler_params=pltpu.CompilerParams(
            collective_id=0, has_side_effects=True, vmem_limit_bytes=32 * 1024 * 1024
        ),
        cost_estimate=pl.CostEstimate(
            flops=4 * heads * rows * rows * HEAD,
            bytes_accessed=2 * (members + 1) * rows * features,
            transcendentals=heads * rows * rows,
        ),
    )(*(pltpu.with_memory_space_constraint(x, pltpu.HBM) for x in (slot_offset, pack_segments, qkv)))
    return out.reshape(seqs * slots, mine * HEAD)


def solution(mesh):
    return jax.shard_map(
        functools.partial(on_device, mesh.shape["seq"], mesh.shape["mp"]),
        mesh=mesh,
        in_specs=(P(None, ("seq", "mp"), None), P(), P()),
        out_specs=P("seq", "mp"),
        check_vma=False,
    )
```
